256 devices in a mesh: aa: 16 (over y, x_lo, core), ba: 8 (over z), ao: 2 (over x_hi).
Axes of the slice: x: 4 (x_hi: 2, x_lo: 2; x = x_hi * 2 + x_lo), y: 4, z: 8, core: 2. Of those that a mesh axis runs over, the one named last changes fastest.
Arguments:
- integrals: float32 [1048576, 256], P(('aa', 'ba')), may hold values from -0.375 to 0.375
- amplitudes: float32 [2048, 512], P(('aa', 'ba'), 'ao'), may hold values from -6 to 6
- row_irrep: int32 [8192], P(('aa', 'ba')), may hold values from 0 to 7
- cd_irrep: int32 [16], replicated, may hold values from 0 to 7, as said below
- cd_order: int32 [2048], replicated, may hold values from 0 to 2047, each once
Outputs:
- ladder: float32 [1048576, 512], P(('aa', 'ba'), 'ao')
The draws below stay inside these ranges and needn't reach their ends.
Inputs may be any that keep to these rules, and one draw needn't show every extreme that they name: cd_order is a permutation of 0 to 2047. `cd_irrep`: every label appears exactly twice.
All inputs are finite; a program needn't handle non-finite values.
Results may differ from the reference program's by a relative error of at most 0.00007.
Values sent between devices are 32-bit elements; how exact they have to be, the bound alone decides.
No kernel may reach another device: no remote copies, remote signals or barrier semaphores. Data moves between devices by JAX's collectives and lax.ppermute only.
A program may use at most 128 MiB of HBM per device.

```python
import jax
import jax.numpy as jnp
from jax import lax

KCD = 2048
NIRREP = 8
BLK = 128
ROWS = 1048576
OCC = 512


def draw_cd_irrep(key, part):
    key = jax.random.fold_in(key, 7)
    return (jax.random.permutation(key, KCD // BLK) % NIRREP).astype(jnp.int32)


def place_ends(values, stream_key, least, largest):
    dims = values.shape
    place = [jax.random.randint(jax.random.fold_in(stream_key, axis), (), 0, dims[axis]) for axis in range(len(dims))]
    values = values.at[tuple(place)].set(least)
    longest = dims.index(max(dims))
    place[longest] = (place[longest] + 1) % dims[longest]
    return values.at[tuple(place)].set(largest)


def levels(rng, shape, pieces, least, top_value):
    factor_of = 1.0
    for axis_at, parts in pieces:
        draws = jax.random.uniform(jax.random.fold_in(jax.random.fold_in(rng, 6), axis_at), (parts,), jnp.float32, least / len(pieces), top_value / len(pieces))
        factor_of = factor_of * jnp.repeat(jnp.exp(draws), shape[axis_at] // parts).reshape((-1,) + (1,) * (len(shape) - 1 - axis_at))
    return factor_of


def scatter_about(own_key, dims, spread, most, shards=(), held_as=jnp.bfloat16):
    entries = jax.random.normal(own_key, dims, jnp.float32) * spread
    if len(shards) > 0:
        entries = levels(own_key, dims, shards, -0.22, 0.18) * entries
    return jnp.clip(entries, min=-most, max=most).astype(held_as)


def setup_inputs(seed: int = 0) -> dict:
    splits = jax.random.split(jax.random.key(seed), 6)
    integrals = scatter_about(splits[0], (ROWS, 2 * BLK), (2 * BLK) ** -0.5, 0.375, ((0, 128),), jnp.float32)
    amplitudes = scatter_about(splits[1], (KCD, OCC), 1.0, 6.0, ((0, 128), (1, 2)), jnp.float32)
    row_irrep = place_ends(jax.random.randint(splits[2], (ROWS // BLK,), 0, NIRREP), jax.random.fold_in(splits[2], 1), 0, NIRREP - 1).astype(jnp.int32)
    cd_irrep = draw_cd_irrep(jax.random.fold_in(splits[5], 71), 0)
    cd_order = jax.random.permutation(splits[4], KCD).astype(jnp.int32)
    return {"integrals": integrals, "amplitudes": amplitudes, "row_irrep": row_irrep, "cd_irrep": cd_irrep, "cd_order": cd_order}


def reference(integrals, amplitudes, row_irrep, cd_irrep, cd_order):
    half_occ = OCC // 2
    mirrored = amplitudes[:, ::-1]
    combined = jnp.concatenate([amplitudes[:, :half_occ] + mirrored[:, :half_occ], mirrored[:, half_occ:] - amplitudes[:, half_occ:]], axis=1)
    sorted_blocks = jnp.argsort(cd_irrep, stable=True).astype(jnp.int32).reshape(NIRREP, 2)
    offsets = jnp.arange(BLK, dtype=jnp.int32)
    columns = (sorted_blocks[:, :, None] * BLK + offsets[None, None, :]).reshape(NIRREP * 2 * BLK)
    amp_rows = jnp.take(cd_order, columns).astype(jnp.int32)
    picked = jnp.take(combined, amp_rows, axis=0).reshape(NIRREP, 2 * BLK, OCC)
    slab_blocks = integrals.reshape(ROWS // BLK, BLK, 2 * BLK)

    def one_block(pair):
        slab, label = pair
        return jnp.dot(slab, picked[label], precision=lax.Precision.HIGHEST, preferred_element_type=jnp.float32)

    result = lax.map(one_block, (slab_blocks, row_irrep.astype(jnp.int32)))
    return result.reshape(ROWS, OCC)
```

```python
import functools

import jax
import jax.numpy as jnp
import numpy as np
from jax import lax
from jax.experimental import pallas as pl
from jax.experimental.pallas import tpu as pltpu
from jax.sharding import PartitionSpec as P

CORE = 8
Z1, Z2, Z7, X1, Y1, Y3 = 1, 2, 7, 16, 32, 96
ROUNDS = ((Z7, Y3), (Z2, Z1), (X1, Y1))

CHUNK = 512


def trade(block, mask):
    return lax.ppermute(block, ("aa", "ba"), [(i, i ^ mask) for i in range(128)])


def slot_bits():
    masks = [m for pair in ROUNDS for m in pair] + [CORE]
    source_of = np.zeros(128, np.int64)
    for slot in range(128):
        for bit, mask in enumerate(masks):
            if slot >> bit & 1:
                source_of[slot] ^= mask
    slot_of = np.argsort(source_of)
    return [int(slot_of[1 << bit]) for bit in range(7)]


def ladder_kernel(slots, cd_irrep, row_irrep, integrals, gathered, out, block_of, a_buf, picked, high, low, o_buf, a_sem, o_sem):
    count = integrals.shape[0] // CHUNK
    block = picked.shape[1] // 16

    def fetch(i):
        at = pl.ds(i * CHUNK, CHUNK)
        return pltpu.make_async_copy(integrals.at[at], a_buf.at[at], a_sem.at[i])

    def flush(i):
        at = pl.ds(i * CHUNK, CHUNK)
        return pltpu.make_async_copy(o_buf.at[at], out.at[at], o_sem.at[i])

    for i in range(count):
        fetch(i).start()

    for s in range(16):
        block_of[s] = -1
    for b in range(16):
        s = cd_irrep[b]
        half = jnp.where(block_of[2 * s] < 0, 0, 1)
        block_of[2 * s + half] = b

    def pick(q, carry):
        base = block_of[q] * block

        def rows(t, carry):
            for k in range(16):
                j = t * 16 + k
                r = slots[base + j]
                picked[0, pl.ds(q * block + j, 1), :] = gathered[pl.ds(r, 1), :]
                picked[1, pl.ds(q * block + j, 1), :] = gathered[pl.ds(r + 16, 1), :]
            return carry

        return lax.fori_loop(0, block // 16, rows, carry)

    lax.fori_loop(0, 16, pick, 0)

    def split(s, carry):
        for c in range(2):
            v = picked[c, pl.ds(s * 2 * block, 2 * block), :]
            hi = v.astype(jnp.bfloat16)
            high[s, :, c * 128 : c * 128 + 128] = hi
            low[s, :, c * 128 : c * 128 + 128] = (v - hi.astype(jnp.float32)).astype(jnp.bfloat16)
        return carry

    lax.fori_loop(0, 8, split, 0)
    dot = functools.partial(jnp.dot, preferred_element_type=jnp.float32)

    def step(i, carry):
        fetch(i).wait()
        for k in range(CHUNK // block):
            at = pl.ds(pl.multiple_of(i * CHUNK + k * block, block), block)
            a = a_buf[at, :]
            a_hi = a.astype(jnp.bfloat16)
            a_lo = (a - a_hi.astype(jnp.float32)).astype(jnp.bfloat16)
            s = row_irrep[i * (CHUNK // block) + k]
            o_buf[at, :] = dot(a_hi, low[s]) + dot(a_lo, high[s]) + dot(a_hi, high[s])
        flush(i).start()
        return carry

    lax.fori_loop(0, count, step, 0)
    for i in range(count):
        flush(i).wait()


def ladder(slots, cd_irrep, row_irrep, integrals, gathered):
    rows = integrals.shape[0]
    smem = pl.BlockSpec(memory_space=pltpu.SMEM)
    hbm = pl.BlockSpec(memory_space=pl.ANY)
    return pl.pallas_call(
        ladder_kernel,
        out_shape=jax.ShapeDtypeStruct((rows, 256), jnp.float32),
        in_specs=[smem, smem, smem, hbm, pl.BlockSpec(memory_space=pltpu.VMEM)],
        out_specs=hbm,
        scratch_shapes=[
            pltpu.SMEM((16,), jnp.int32),
            pltpu.VMEM((rows, 256), jnp.float32),
            pltpu.VMEM((2, 2048, 128), jnp.float32),
            pltpu.VMEM((8, 256, 256), jnp.bfloat16),
            pltpu.VMEM((8, 256, 256), jnp.bfloat16),
            pltpu.VMEM((rows, 256), jnp.float32),
            pltpu.SemaphoreType.DMA((rows // CHUNK,)),
            pltpu.SemaphoreType.DMA((rows // CHUNK,)),
        ],
        compiler_params=pltpu.CompilerParams(vmem_limit_bytes=40 << 20),
    )(slots, cd_irrep, row_irrep, integrals, gathered)


def on_device(integrals, amplitudes, row_irrep, cd_irrep, cd_order):
    me = lax.axis_index(("aa", "ba"))
    relative = (cd_order >> 4) ^ me
    slot = jnp.zeros_like(cd_order)
    for bit, image in enumerate(slot_bits()):
        slot = slot ^ jnp.where(relative >> bit & 1 == 1, image, 0)
    slots = slot * 32 + (cd_order & 15)

    parity = (1 - 2 * lax.axis_index("ao")).astype(jnp.float32)
    partner = lax.ppermute(amplitudes, "ao", [(0, 1), (1, 0)])
    block = partner[:, ::-1] + parity * amplitudes
    block = jnp.concatenate([block[:, :128], block[:, 128:]])
    for a, b in ROUNDS:
        both = trade(block, a ^ b)
        block = jnp.concatenate([block, trade(block, a), trade(block, b), both])
    block = jnp.concatenate([block, trade(block, CORE)])
    return ladder(slots, cd_irrep, row_irrep, integrals, block)


def solution(mesh):
    placed = (P(("aa", "ba"), None), P(("aa", "ba"), "ao"), P(("aa", "ba")), P(), P())
    return jax.shard_map(
        on_device, mesh=mesh, in_specs=placed, out_specs=P(("aa", "ba"), "ao"), check_vma=False
    )
```

```python
import functools

import jax
import jax.numpy as jnp
import numpy as np
from jax import lax
from jax.experimental import pallas as pl
from jax.experimental.pallas import tpu as pltpu
from jax.sharding import PartitionSpec as P

CORE = 8
Z1, Z2, Z7, X1, Y1, Y3 = 1, 2, 7, 16, 32, 96
STEPS = ((Z7, Z7), (Z2, Z2), (Y3, X1), (Z1, Y1), (X1, Z1), (Y1, Y3))

CHUNK = 512
STRIDE = 2048


def trade(block, masks):
    return lax.ppermute(block, ("aa", "ba"), [(i, i ^ masks[i // CORE % 2]) for i in range(128)])


def slot_bits(core):
    masks = [step[core] for step in STEPS]
    source_of = {}
    for slot in range(64):
        source = 0
        for bit, mask in enumerate(masks):
            if slot >> bit & 1:
                source ^= mask
        source_of[source] = slot
    return [0 if 1 << bit == CORE else source_of[1 << bit] for bit in range(7)]


def ladder_kernel(slots, cd_irrep, row_irrep, a_hi, a_lo, *rest):
    pieces, (out, block_of, gathered, picked, high, low, o_buf, o_sem) = rest[:8], rest[8:]
    rows = out.shape[0]
    block = picked.shape[1] // 16
    size = pieces[0].shape[0]

    def flush(i):
        at = pl.ds(i * CHUNK, CHUNK)
        return pltpu.make_async_copy(o_buf.at[at], out.at[at], o_sem.at[i])

    for i, piece in enumerate(pieces):
        gathered[i * size : (i + 1) * size, :] = piece[...]
    for s in range(16):
        block_of[s] = -1
    for b in range(16):
        s = cd_irrep[b]
        half = jnp.where(block_of[2 * s] < 0, 0, 1)
        block_of[2 * s + half] = b

    def pick(q, carry):
        base = block_of[q] * block

        def some(t, carry):
            for k in range(16):
                j = t * 16 + k
                r = slots[base + j]
                picked[0, pl.ds(q * block + j, 1), :] = gathered[pl.ds(r, 1), :]
                picked[1, pl.ds(q * block + j, 1), :] = gathered[pl.ds(r + 16, 1), :]
            return carry

        return lax.fori_loop(0, block // 16, some, carry)

    lax.fori_loop(0, 16, pick, 0)

    def split(s, carry):
        for c in range(2):
            v = picked[c, pl.ds(s * 2 * block, 2 * block), :]
            hi = v.astype(jnp.bfloat16)
            high[s, :, c * 128 : c * 128 + 128] = hi
            low[s, :, c * 128 : c * 128 + 128] = (v - hi.astype(jnp.float32)).astype(jnp.bfloat16)
        return carry

    lax.fori_loop(0, 8, split, 0)

    def step(i, carry):
        for k in range(STRIDE // block):
            at = pl.ds(pl.multiple_of(i * STRIDE + k * block, block), block)
            s = row_irrep[i * (STRIDE // block) + k]
            hi, b_hi = a_hi[at, :], high[s]
            left = jnp.concatenate([hi, a_lo[at, :], hi], axis=1)
            right = jnp.concatenate([low[s], b_hi, b_hi], axis=0)
            o_buf[at, :] = jnp.dot(left, right, preferred_element_type=jnp.float32)
            done = (k + 1) * block - CHUNK
            if done > 0 and done % CHUNK == 0:
                flush(i * (STRIDE // CHUNK) + done // CHUNK - 1).start()
        flush((i + 1) * (STRIDE // CHUNK) - 1).start()
        return carry

    lax.fori_loop(0, rows // STRIDE, step, 0)
    for i in range(rows // CHUNK):
        flush(i).wait()


def ladder(slots, cd_irrep, row_irrep, a_hi, a_lo, pieces):
    rows = a_hi.shape[0]
    smem = pl.BlockSpec(memory_space=pltpu.SMEM)
    vmem = pl.BlockSpec(memory_space=pltpu.VMEM)
    return pl.pallas_call(
        ladder_kernel,
        out_shape=jax.ShapeDtypeStruct((rows, 256), jnp.float32),
        in_specs=[smem] * 3 + [vmem] * (2 + len(pieces)),
        out_specs=pl.BlockSpec(memory_space=pl.ANY),
        scratch_shapes=[
            pltpu.SMEM((16,), jnp.int32),
            pltpu.VMEM((4096, 128), jnp.float32),
            pltpu.VMEM((2, 2048, 128), jnp.float32),
            pltpu.VMEM((8, 256, 256), jnp.bfloat16),
            pltpu.VMEM((8, 256, 256), jnp.bfloat16),
            pltpu.VMEM((rows, 256), jnp.float32),
            pltpu.SemaphoreType.DMA((rows // CHUNK,)),
        ],
        compiler_params=pltpu.CompilerParams(vmem_limit_bytes=32 << 20),
    )(slots, cd_irrep, row_irrep, a_hi, a_lo, *pieces)


def on_device(integrals, amplitudes, row_irrep, cd_irrep, cd_order):
    rounded = lax.reduce_precision(integrals, exponent_bits=8, mantissa_bits=7)
    a_hi = rounded.astype(jnp.bfloat16)
    a_lo = (integrals - rounded).astype(jnp.bfloat16)

    me = lax.axis_index(("aa", "ba"))
    source = cd_order >> 4
    relative = source ^ me
    source_core = source >> 3 & 1
    slot = (relative >> 3 & 1) << 6
    for bit, (zero, one) in enumerate(zip(slot_bits(0), slot_bits(1))):
        image = jnp.where(source_core == 1, one, zero)
        slot = slot ^ jnp.where(relative >> bit & 1 == 1, image, 0)
    slots = slot * 32 + (cd_order & 15)

    parity = (1 - 2 * lax.axis_index("ao")).astype(jnp.float32)
    partner = lax.ppermute(amplitudes, "ao", [(0, 1), (1, 0)])
    partner, a_hi, a_lo = lax.optimization_barrier((partner, a_hi, a_lo))
    block = partner[:, ::-1] + parity * amplitudes
    block = jnp.concatenate([block[:, :128], block[:, 128:]])
    for masks in STEPS[:-2]:
        block = lax.optimization_barrier(jnp.concatenate([block, trade(block, masks)]))
    a, b = STEPS[-2:]
    both = tuple(p ^ q for p, q in zip(a, b))
    pieces = [block, trade(block, a), trade(block, b), trade(block, both)]
    pieces += [trade(piece, (CORE, CORE)) for piece in pieces]
    return ladder(slots, cd_irrep, row_irrep, a_hi, a_lo, pieces)


def solution(mesh):
    placed = (P(("aa", "ba"), None), P(("aa", "ba"), "ao"), P(("aa", "ba")), P(), P())
    return jax.shard_map(
        on_device, mesh=mesh, in_specs=placed, out_specs=P(("aa", "ba"), "ao"), check_vma=False
    )
```

```python
import jax
import jax.numpy as jnp
from jax import lax
from jax.experimental import pallas as pl
from jax.experimental.pallas import tpu as pltpu
from jax.sharding import PartitionSpec as P

CORE = 8
Z1, Z2, Z6, X1, Y1, Y3 = 1, 2, 6, 16, 32, 96
STEPS = ((Z6, Z6), (Z2, Z2), (Y3, X1), (Z1, Y1), (X1, Z1), (Y1, Y3))

CHUNK = 512
STRIDE = 2048


def trade(block, masks):
    route = [(i, i ^ masks[i // CORE % 2]) for i in range(128)]
    return lax.ppermute(block, ("aa", "ba"), [(i, j) for i, j in route if i != j])


def trade_raw(amplitudes, masks):
    route = [(i, i ^ masks[i // 2 // CORE % 2]) for i in range(256)]
    return lax.ppermute(amplitudes, ("aa", "ba", "ao"), [(i, j) for i, j in route if i != j])


def slot_bits(core):
    masks = [step[core] for step in STEPS]
    source_of = {}
    for slot in range(64):
        source = 0
        for bit, mask in enumerate(masks):
            if slot >> bit & 1:
                source ^= mask
        source_of[source] = slot
    return [0 if 1 << bit == CORE else source_of[1 << bit] for bit in range(7)]


def ladder_kernel(labels, integrals, *rest):
    pieces, (out, block_of, a_buf, gathered, picked, high, low, o_buf, a_sem, o_sem) = rest[:8], rest[8:]
    rows = out.shape[0]
    block = picked.shape[0] // 32
    size = pieces[0].shape[0]
    pairs, row_blocks = 16 * block, rows // block

    def fetch(i):
        at = pl.ds(i * STRIDE, STRIDE)
        return pltpu.make_async_copy(integrals.at[at], a_buf.at[at], a_sem.at[i])

    def flush(i):
        at = pl.ds(i * CHUNK, CHUNK)
        return pltpu.make_async_copy(o_buf.at[at], out.at[at], o_sem.at[i])

    for i in range(rows // STRIDE):
        fetch(i).start()
    for i, piece in enumerate(pieces):
        gathered[i * size : (i + 1) * size, :] = piece[...]
    for s in range(16):
        block_of[s] = -1
    for b in range(16):
        s = labels[pairs + row_blocks + b]
        half = jnp.where(block_of[2 * s] < 0, 0, 1)
        block_of[2 * s + half] = b

    def pick(q, carry):
        base = block_of[q] * block

        for j in range(block):
            row = pl.multiple_of(labels[base + j], 2)
            picked[pl.ds(pl.multiple_of((q * block + j) * 2, 2), 2), :] = gathered[pl.ds(row, 2), :]
        return carry

    lax.fori_loop(0, 16, pick, 0)

    def split(s, carry):
        for c in range(2):
            v = picked[pl.ds(s * 4 * block + c, 2 * block, stride=2), :]
            hi = v.astype(jnp.bfloat16)
            high[s, :, c * 128 : c * 128 + 128] = hi
            low[s, :, c * 128 : c * 128 + 128] = (v - hi.astype(jnp.float32)).astype(jnp.bfloat16)
        return carry

    lax.fori_loop(0, 8, split, 0)

    def step(i, carry):
        fetch(i).wait()
        for k in range(STRIDE // block):
            at = pl.ds(pl.multiple_of(i * STRIDE + k * block, block), block)
            s = labels[pairs + i * (STRIDE // block) + k]
            a, b_hi = a_buf[at, :], high[s]
            a_hi = a.astype(jnp.bfloat16)
            a_lo = (a - a_hi.astype(jnp.float32)).astype(jnp.bfloat16)
            left = jnp.concatenate([a_hi, a_lo, a_hi], axis=1)
            right = jnp.concatenate([low[s], b_hi, b_hi], axis=0)
            o_buf[at, :] = jnp.dot(left, right, preferred_element_type=jnp.float32)
            done = (k + 1) * block - CHUNK
            if done > 0 and done % CHUNK == 0:
                flush(i * (STRIDE // CHUNK) + done // CHUNK - 1).start()
        flush((i + 1) * (STRIDE // CHUNK) - 1).start()
        return carry

    lax.fori_loop(0, rows // STRIDE, step, 0)
    for i in range(rows // CHUNK):
        flush(i).wait()


def ladder(labels, integrals, pieces):
    rows = integrals.shape[0]
    smem = pl.BlockSpec(memory_space=pltpu.SMEM)
    vmem = pl.BlockSpec(memory_space=pltpu.VMEM)
    hbm = pl.BlockSpec(memory_space=pl.ANY)
    return pl.pallas_call(
        ladder_kernel,
        out_shape=jax.ShapeDtypeStruct((rows, 256), jnp.float32),
        in_specs=[smem, hbm] + [vmem] * len(pieces),
        out_specs=hbm,
        scratch_shapes=[
            pltpu.SMEM((16,), jnp.int32),
            pltpu.VMEM((rows, 256), jnp.float32),
            pltpu.VMEM((4096, 128), jnp.float32),
            pltpu.VMEM((4096, 128), jnp.float32),
            pltpu.VMEM((8, 256, 256), jnp.bfloat16),
            pltpu.VMEM((8, 256, 256), jnp.bfloat16),
            pltpu.VMEM((rows, 256), jnp.float32),
            pltpu.SemaphoreType.DMA((rows // STRIDE,)),
            pltpu.SemaphoreType.DMA((rows // CHUNK,)),
        ],
        compiler_params=pltpu.CompilerParams(vmem_limit_bytes=48 << 20),
    )(labels, integrals, *pieces)


def on_device(integrals, amplitudes, row_irrep, cd_irrep, cd_order):
    me = lax.axis_index(("aa", "ba"))
    source = cd_order >> 4
    relative = source ^ me
    slot = (relative >> 3 & 1) << 6
    for bit, (zero, one) in enumerate(zip(slot_bits(0), slot_bits(1))):
        image = jnp.where(source >> 3 & 1 == 1, one, zero)
        slot = slot ^ jnp.where(relative >> bit & 1 == 1, image, 0)
    labels = jnp.concatenate([slot * 32 + (cd_order & 15) * 2, row_irrep, cd_irrep])

    parity = (1 - 2 * lax.axis_index("ao")).astype(jnp.float32)
    partner = trade_raw(amplitudes, (1, 1))
    block = (partner[:, ::-1] + parity * amplitudes).reshape(-1, 128)
    for masks in STEPS[0:-2]:
        block = lax.optimization_barrier(jnp.concatenate([block, trade(block, masks)]))
    block, labels = lax.optimization_barrier((block, labels))
    a, b = STEPS[-2:]
    both = tuple(p ^ q for p, q in zip(a, b))
    pieces = [block, trade(block, a), trade(block, b), trade(block, both)]
    pieces += [trade(piece, (CORE, CORE)) for piece in pieces]
    return ladder(labels, integrals, pieces)


def solution(mesh):
    placed = (P(("aa", "ba"), None), P(("aa", "ba"), "ao"), P(("aa", "ba")), P(), P())
    return jax.shard_map(
        on_device, mesh=mesh, in_specs=placed, out_specs=P(("aa", "ba"), "ao"), check_vma=False
    )
```

```python
import jax
import jax.numpy as jnp
from jax import lax
from jax.experimental import pallas as pl
from jax.experimental.pallas import tpu as pltpu
from jax.sharding import PartitionSpec as P

CORE = 8
Z1, Z2, Z6, X1, Y1, Y3 = 1, 2, 6, 16, 32, 96
STEPS = ((Z6, Z6), (Z2, Z2), (Y3, X1), (Z1, Y1), (X1, Z1), (Y1, Y3))

CHUNK = 512
STRIDE = 2048


def trade(block, masks):
    route = [(i, i ^ masks[i // CORE % 2]) for i in range(128)]
    return lax.ppermute(block, ("aa", "ba"), [(i, j) for i, j in route if i != j])


def trade_raw(amplitudes, masks):
    route = [(i, i ^ masks[i // 2 // CORE % 2]) for i in range(256)]
    return lax.ppermute(amplitudes, ("aa", "ba", "ao"), [(i, j) for i, j in route if i != j])


def slot_bits(core):
    masks = [step[core] for step in STEPS]
    source_of = {}
    for slot in range(64):
        source = 0
        for bit, mask in enumerate(masks):
            if slot >> bit & 1:
                source ^= mask
        source_of[source] = slot
    return [0 if 1 << bit == CORE else source_of[1 << bit] for bit in range(7)]


def ladder_kernel(labels, integrals, *rest):
    pieces, (out, block_of, a_buf, gathered, picked, high, low, o_buf, a_sem, o_sem) = rest[:-10], rest[-10:]
    rows = out.shape[0]
    block = picked.shape[0] // 32
    size = pieces[0].shape[0]
    pairs, row_blocks = 16 * block, rows // block

    def fetch(i):
        at = pl.ds(i * STRIDE, STRIDE)
        return pltpu.make_async_copy(integrals.at[at], a_buf.at[at], a_sem.at[i])

    def flush(i):
        at = pl.ds(i * CHUNK, CHUNK)
        return pltpu.make_async_copy(o_buf.at[at], out.at[at], o_sem.at[i])

    for i in range(rows // STRIDE):
        fetch(i).start()
    for i, piece in enumerate(pieces):
        gathered[i * size : (i + 1) * size, :] = piece[...]
    for s in range(16):
        block_of[s] = -1
    for b in range(16):
        s = labels[pairs + row_blocks + b]
        half = jnp.where(block_of[2 * s] < 0, 0, 1)
        block_of[2 * s + half] = b

    def pick(q, carry):
        base = block_of[q] * block

        for j in range(block):
            row = pl.multiple_of(labels[base + j], 2)
            picked[pl.ds(pl.multiple_of((q * block + j) * 2, 2), 2), :] = gathered[pl.ds(row, 2), :]
        return carry

    lax.fori_loop(0, 16, pick, 0)

    def split(s, carry):
        for c in range(2):
            v = picked[pl.ds(s * 4 * block + c, 2 * block, stride=2), :]
            hi = v.astype(jnp.bfloat16)
            high[s, :, c * 128 : c * 128 + 128] = hi
            low[s, :, c * 128 : c * 128 + 128] = (v - hi.astype(jnp.float32)).astype(jnp.bfloat16)
        return carry

    lax.fori_loop(0, 8, split, 0)

    def step(i, carry):
        fetch(i).wait()
        for k in range(STRIDE // block):
            at = pl.ds(pl.multiple_of(i * STRIDE + k * block, block), block)
            s = labels[pairs + i * (STRIDE // block) + k]
            a, b_hi = a_buf[at, :], high[s]
            a_hi = a.astype(jnp.bfloat16)
            a_lo = (a - a_hi.astype(jnp.float32)).astype(jnp.bfloat16)
            left = jnp.concatenate([a_hi, a_lo, a_hi], axis=1)
            right = jnp.concatenate([low[s], b_hi, b_hi], axis=0)
            o_buf[at, :] = jnp.dot(left, right, preferred_element_type=jnp.float32)
            done = (k + 1) * block - CHUNK
            if done > 0 and done % CHUNK == 0:
                flush(i * (STRIDE // CHUNK) + done // CHUNK - 1).start()
        flush((i + 1) * (STRIDE // CHUNK) - 1).start()
        return carry

    lax.fori_loop(0, rows // STRIDE, step, 0)
    for i in range(rows // CHUNK):
        flush(i).wait()


def ladder(labels, integrals, pieces):
    rows = integrals.shape[0]
    smem = pl.BlockSpec(memory_space=pltpu.SMEM)
    vmem = pl.BlockSpec(memory_space=pltpu.VMEM)
    hbm = pl.BlockSpec(memory_space=pl.ANY)
    return pl.pallas_call(
        ladder_kernel,
        out_shape=jax.ShapeDtypeStruct((rows, 256), jnp.float32),
        in_specs=[smem, hbm] + [vmem] * len(pieces),
        out_specs=hbm,
        scratch_shapes=[
            pltpu.SMEM((16,), jnp.int32),
            pltpu.VMEM((rows, 256), jnp.float32),
            pltpu.VMEM((4096, 128), jnp.float32),
            pltpu.VMEM((4096, 128), jnp.float32),
            pltpu.VMEM((8, 256, 256), jnp.bfloat16),
            pltpu.VMEM((8, 256, 256), jnp.bfloat16),
            pltpu.VMEM((rows, 256), jnp.float32),
            pltpu.SemaphoreType.DMA((rows // STRIDE,)),
            pltpu.SemaphoreType.DMA((rows // CHUNK,)),
        ],
        compiler_params=pltpu.CompilerParams(vmem_limit_bytes=48 << 20),
    )(labels, integrals, *pieces)


def on_device(integrals, amplitudes, row_irrep, cd_irrep, cd_order):
    me = lax.axis_index(("aa", "ba"))
    source = cd_order >> 4
    relative = source ^ me
    slot = (relative >> 3 & 1) << 6
    for bit, (zero, one) in enumerate(zip(slot_bits(0), slot_bits(1))):
        image = jnp.where(source >> 3 & 1 == 1, one, zero)
        slot = slot ^ jnp.where(relative >> bit & 1 == 1, image, 0)
    labels = jnp.concatenate([slot * 32 + (cd_order & 15) * 2, row_irrep, cd_irrep])

    parity = (1 - 2 * lax.axis_index("ao")).astype(jnp.float32)
    partner = trade_raw(amplitudes, (1, 1))
    block = (partner[:, ::-1] + parity * amplitudes).reshape(-1, 128)
    for masks in STEPS[:-3]:
        block = lax.optimization_barrier(jnp.concatenate([block, trade(block, masks)]))
    block, labels = lax.optimization_barrier((block, labels))
    a, b = STEPS[-2:]
    both = tuple(p ^ q for p, q in zip(a, b))
    later = trade(block, STEPS[-3])
    early = [trade(block, masks) for masks in (a, b, both)]
    late = [trade(later, masks) for masks in (a, b, both)]
    *early, late[2] = lax.optimization_barrier((*early, late[2]))
    pieces = [block, later] + [piece for pair in zip(early, late) for piece in pair]
    pieces += [trade(piece, (CORE, CORE)) for piece in pieces]
    return ladder(labels, integrals, pieces)


def solution(mesh):
    placed = (P(("aa", "ba"), None), P(("aa", "ba"), "ao"), P(("aa", "ba")), P(), P())
    return jax.shard_map(
        on_device, mesh=mesh, in_specs=placed, out_specs=P(("aa", "ba"), "ao"), check_vma=False
    )
```

```python
import jax
import jax.numpy as jnp
from jax import lax
from jax.experimental import pallas as pl
from jax.experimental.pallas import tpu as pltpu
from jax.sharding import PartitionSpec as P

CORE = 8
Z1, Z2, Z6, X1, Y1, Y3 = 1, 2, 6, 16, 32, 96
STEPS = ((Z6, Z6), (Z2, Z2), (Y3, X1), (Z1, Y1), (X1, Z1), (Y1, Y3))

CHUNK = 512
STRIDE = 4096


def trade(block, masks):
    route = [(i, i ^ masks[i // CORE % 2]) for i in range(128)]
    return lax.ppermute(block, ("aa", "ba"), [(i, j) for i, j in route if i != j])


def trade_raw(amplitudes, masks):
    route = [(i, i ^ masks[i // 2 // CORE % 2]) for i in range(256)]
    return lax.ppermute(amplitudes, ("aa", "ba", "ao"), [(i, j) for i, j in route if i != j])


def slot_bits(core):
    masks = [step[core] for step in STEPS]
    source_of = {}
    for slot in range(64):
        source = 0
        for bit, mask in enumerate(masks):
            if slot >> bit & 1:
                source ^= mask
        source_of[source] = slot
    return [0 if 1 << bit == CORE else source_of[1 << bit] for bit in range(7)]


def ladder_kernel(labels, integrals, *rest):
    pieces, (out, block_of, a_buf, gathered, picked, high, low, o_buf, a_sem, o_sem) = rest[:-10], rest[-10:]
    rows = out.shape[0]
    block = picked.shape[0] // 32
    size = pieces[0].shape[0]
    pairs, row_blocks = 16 * block, rows // block

    def fetch(i):
        at = pl.ds(i * STRIDE, STRIDE)
        return pltpu.make_async_copy(integrals.at[at], a_buf.at[at], a_sem.at[i])

    def flush(i):
        at = pl.ds(i * CHUNK, CHUNK)
        return pltpu.make_async_copy(o_buf.at[at], out.at[at], o_sem.at[i])

    for i in range(rows // STRIDE):
        fetch(i).start()
    for i, piece in enumerate(pieces):
        gathered[i * size : (i + 1) * size, :] = piece[...]
    for s in range(16):
        block_of[s] = -1
    for b in range(16):
        s = labels[pairs + row_blocks + b]
        half = jnp.where(block_of[2 * s] < 0, 0, 1)
        block_of[2 * s + half] = b

    def pick(q, carry):
        base = block_of[q] * block

        for j in range(block):
            row = pl.multiple_of(labels[base + j], 2)
            picked[pl.ds(pl.multiple_of((q * block + j) * 2, 2), 2), :] = gathered[pl.ds(row, 2), :]
        return carry

    lax.fori_loop(0, 16, pick, 0)

    def split(s, carry):
        for c in range(2):
            v = picked[pl.ds(s * 4 * block + c, 2 * block, stride=2), :]
            hi = v.astype(jnp.bfloat16)
            high[s, :, c * 128 : c * 128 + 128] = hi
            low[s, :, c * 128 : c * 128 + 128] = (v - hi.astype(jnp.float32)).astype(jnp.bfloat16)
        return carry

    lax.fori_loop(0, 8, split, 0)

    def step(i, carry):
        fetch(i).wait()
        for k in range(STRIDE // block):
            at = pl.ds(pl.multiple_of(i * STRIDE + k * block, block), block)
            s = labels[pairs + i * (STRIDE // block) + k]
            a, b_hi = a_buf[at, :], high[s]
            a_hi = a.astype(jnp.bfloat16)
            a_lo = (a - a_hi.astype(jnp.float32)).astype(jnp.bfloat16)
            left = jnp.concatenate([a_hi, a_lo, a_hi], axis=1)
            right = jnp.concatenate([low[s], b_hi, b_hi], axis=0)
            o_buf[at, :] = jnp.dot(left, right, preferred_element_type=jnp.float32)
            done = (k + 1) * block - CHUNK
            if done > 0 and done % CHUNK == 0:
                flush(i * (STRIDE // CHUNK) + done // CHUNK - 1).start()
        flush((i + 1) * (STRIDE // CHUNK) - 1).start()
        return carry

    lax.fori_loop(0, rows // STRIDE, step, 0)
    for i in range(rows // CHUNK):
        flush(i).wait()


def ladder(labels, integrals, pieces):
    rows = integrals.shape[0]
    smem = pl.BlockSpec(memory_space=pltpu.SMEM)
    vmem = pl.BlockSpec(memory_space=pltpu.VMEM)
    hbm = pl.BlockSpec(memory_space=pl.ANY)
    return pl.pallas_call(
        ladder_kernel,
        out_shape=jax.ShapeDtypeStruct((rows, 256), jnp.float32),
        in_specs=[smem, hbm] + [vmem] * len(pieces),
        out_specs=hbm,
        scratch_shapes=[
            pltpu.SMEM((16,), jnp.int32),
            pltpu.VMEM((rows, 256), jnp.float32),
            pltpu.VMEM((4096, 128), jnp.float32),
            pltpu.VMEM((4096, 128), jnp.float32),
            pltpu.VMEM((8, 256, 256), jnp.bfloat16),
            pltpu.VMEM((8, 256, 256), jnp.bfloat16),
            pltpu.VMEM((rows, 256), jnp.float32),
            pltpu.SemaphoreType.DMA((rows // STRIDE,)),
            pltpu.SemaphoreType.DMA((rows // CHUNK,)),
        ],
        compiler_params=pltpu.CompilerParams(vmem_limit_bytes=48 << 20),
    )(labels, integrals, *pieces)


def on_device(integrals, amplitudes, row_irrep, cd_irrep, cd_order):
    me = lax.axis_index(("aa", "ba"))
    source = cd_order >> 4
    relative = source ^ me
    slot = (relative >> 3 & 1) << 6
    for bit, (zero, one) in enumerate(zip(slot_bits(0), slot_bits(1))):
        image = jnp.where(source >> 3 & 1 == 1, one, zero)
        slot = slot ^ jnp.where(relative >> bit & 1 == 1, image, 0)
    labels = jnp.concatenate([slot * 32 + (cd_order & 15) * 2, row_irrep, cd_irrep])

    parity = (1 - 2 * lax.axis_index("ao")).astype(jnp.float32)
    partner = trade_raw(amplitudes, (1, 1))
    partner, scaled, labels = lax.optimization_barrier((partner, parity * amplitudes, labels))
    block = (partner[:, ::-1] + scaled).reshape(-1, 128)
    for masks in STEPS[:-3]:
        block = lax.optimization_barrier(jnp.concatenate([block, trade(block, masks)]))
    a, b = STEPS[-2:]
    both = tuple(p ^ q for p, q in zip(a, b))
    later = trade(block, STEPS[-3])
    early = [trade(block, masks) for masks in (a, b, both)]
    late = [trade(later, masks) for masks in (a, b, both)]
    *early, late[2] = lax.optimization_barrier((*early, late[2]))
    pieces = [block, later] + [piece for pair in zip(early, late) for piece in pair]
    pieces += [trade(piece, (CORE, CORE)) for piece in pieces]
    return ladder(labels, integrals, pieces)


def solution(mesh):
    placed = (P(("aa", "ba"), None), P(("aa", "ba"), "ao"), P(("aa", "ba")), P(), P())
    return jax.shard_map(
        on_device, mesh=mesh, in_specs=placed, out_specs=P(("aa", "ba"), "ao"), check_vma=False
    )
```

```python
import jax
import jax.numpy as jnp
from jax import lax
from jax.experimental import pallas as pl
from jax.experimental.pallas import tpu as pltpu
from jax.sharding import PartitionSpec as P

CORE = 8
Z1, Z2, Z6, X1, Y1, Y3 = 1, 2, 6, 16, 32, 96
STEPS = ((Z6, Z6), (Z2, Z2), (Y3, X1), (Z1, Y1), (X1, Z1), (Y1, Y3))

CHUNK = 512
STRIDE = 4096


def trade(block, masks):
    route = [(i, i ^ masks[i // CORE % 2]) for i in range(128)]
    return lax.ppermute(block, ("aa", "ba"), [(i, j) for i, j in route if i != j])


def trade_raw(amplitudes, masks):
    route = [(i, i ^ masks[i // 2 // CORE % 2]) for i in range(256)]
    return lax.ppermute(amplitudes, ("aa", "ba", "ao"), [(i, j) for i, j in route if i != j])


def slot_bits(core):
    masks = [step[core] for step in STEPS]
    source_of = {}
    for slot in range(64):
        source = 0
        for bit, mask in enumerate(masks):
            if slot >> bit & 1:
                source ^= mask
        source_of[source] = slot
    return [0 if 1 << bit == CORE else source_of[1 << bit] for bit in range(7)]


def ladder_kernel(labels, integrals, *rest):
    pieces, (out, block_of, a_buf, gathered, picked, high, low, o_buf, a_sem, o_sem) = rest[:-10], rest[-10:]
    rows = out.shape[0]
    block = picked.shape[0] // 32
    size = pieces[0].shape[0]
    pairs, row_blocks = 16 * block, rows // block

    def fetch(i):
        at = pl.ds(i * STRIDE, STRIDE)
        return pltpu.make_async_copy(integrals.at[at], a_buf.at[at], a_sem.at[i])

    def flush(i):
        at = pl.ds(i * CHUNK, CHUNK)
        return pltpu.make_async_copy(o_buf.at[at], out.at[at], o_sem.at[i])

    for i in range(rows // STRIDE):
        fetch(i).start()
    for i, piece in enumerate(pieces):
        gathered[i * size : (i + 1) * size, :] = piece[...]
    for s in range(16):
        block_of[s] = -1
    for b in range(16):
        s = labels[pairs + row_blocks + b]
        half = jnp.where(block_of[2 * s] < 0, 0, 1)
        block_of[2 * s + half] = b

    def pick(q, carry):
        base = block_of[q] * block

        for j in range(block):
            row = pl.multiple_of(labels[base + j], 2)
            picked[pl.ds(pl.multiple_of((q * block + j) * 2, 2), 2), :] = gathered[pl.ds(row, 2), :]
        return carry

    lax.fori_loop(0, 16, pick, 0)

    def split(s, carry):
        for c in range(2):
            v = picked[pl.ds(s * 4 * block + c, 2 * block, stride=2), :]
            hi = v.astype(jnp.bfloat16)
            high[s, :, c * 128 : c * 128 + 128] = hi
            low[s, :, c * 128 : c * 128 + 128] = (v - hi.astype(jnp.float32)).astype(jnp.bfloat16)
        return carry

    lax.fori_loop(0, 8, split, 0)

    def step(i, carry):
        fetch(i).wait()
        for k in range(STRIDE // block):
            at = pl.ds(pl.multiple_of(i * STRIDE + k * block, block), block)
            s = labels[pairs + i * (STRIDE // block) + k]
            a, b_hi = a_buf[at, :], high[s]
            a_hi = a.astype(jnp.bfloat16)
            a_lo = (a - a_hi.astype(jnp.float32)).astype(jnp.bfloat16)
            left = jnp.concatenate([a_hi, a_lo, a_hi], axis=1)
            right = jnp.concatenate([low[s], b_hi, b_hi], axis=0)
            o_buf[at, :] = jnp.dot(left, right, preferred_element_type=jnp.float32)
            done = (k + 1) * block - CHUNK
            if done > 0 and done % CHUNK == 0:
                flush(i * (STRIDE // CHUNK) + done // CHUNK - 1).start()
        flush((i + 1) * (STRIDE // CHUNK) - 1).start()
        return carry

    lax.fori_loop(0, rows // STRIDE, step, 0)
    for i in range(rows // CHUNK):
        flush(i).wait()


def ladder(labels, integrals, pieces):
    rows = integrals.shape[0]
    smem = pl.BlockSpec(memory_space=pltpu.SMEM)
    vmem = pl.BlockSpec(memory_space=pltpu.VMEM)
    hbm = pl.BlockSpec(memory_space=pl.ANY)
    return pl.pallas_call(
        ladder_kernel,
        out_shape=jax.ShapeDtypeStruct((rows, 256), jnp.float32),
        in_specs=[smem, hbm] + [vmem] * len(pieces),
        out_specs=hbm,
        scratch_shapes=[
            pltpu.SMEM((16,), jnp.int32),
            pltpu.VMEM((rows, 256), jnp.float32),
            pltpu.VMEM((4096, 128), jnp.float32),
            pltpu.VMEM((4096, 128), jnp.float32),
            pltpu.VMEM((8, 256, 256), jnp.bfloat16),
            pltpu.VMEM((8, 256, 256), jnp.bfloat16),
            pltpu.VMEM((rows, 256), jnp.float32),
            pltpu.SemaphoreType.DMA((rows // STRIDE,)),
            pltpu.SemaphoreType.DMA((rows // CHUNK,)),
        ],
        compiler_params=pltpu.CompilerParams(vmem_limit_bytes=48 << 20),
    )(labels, integrals, *pieces)


def on_device(integrals, amplitudes, row_irrep, cd_irrep, cd_order):
    me = lax.axis_index(("aa", "ba"))
    source = cd_order >> 4
    relative = source ^ me
    slot = (relative >> 3 & 1) << 6
    for bit, (zero, one) in enumerate(zip(slot_bits(0), slot_bits(1))):
        image = jnp.where(source >> 3 & 1 == 1, one, zero)
        slot = slot ^ jnp.where(relative >> bit & 1 == 1, image, 0)
    labels = jnp.concatenate([slot * 32 + (cd_order & 15) * 2, row_irrep, cd_irrep])

    parity = (1 - 2 * lax.axis_index("ao")).astype(jnp.float32)
    partner = trade_raw(amplitudes, (1, 1))
    partner, scaled, labels = lax.optimization_barrier((partner, parity * amplitudes, labels))
    block = (partner[:, ::-1] + scaled).reshape(-1, 128)
    for masks in STEPS[:-3]:
        block = lax.optimization_barrier(jnp.concatenate([block, trade(block, masks)]))
    a, b = STEPS[-2:]
    both = tuple(p ^ q for p, q in zip(a, b))
    later = trade(block, STEPS[-3])
    early = [trade(block, masks) for masks in (a, b, both)]
    late = [trade(later, masks) for masks in (a, b, both)]
    *early, late[2] = lax.optimization_barrier((*early, late[2]))
    block, late[0] = lax.optimization_barrier((block, late[0]))
    pieces = [block, later] + [piece for pair in zip(early, late) for piece in pair]
    pieces += [trade(piece, (CORE, CORE)) for piece in pieces]
    return ladder(labels, integrals, pieces)


def solution(mesh):
    placed = (P(("aa", "ba"), None), P(("aa", "ba"), "ao"), P(("aa", "ba")), P(), P())
    return jax.shard_map(
        on_device, mesh=mesh, in_specs=placed, out_specs=P(("aa", "ba"), "ao"), check_vma=False
    )
```
